32 devices in a mesh: tm: 4 (over y, x), rows: 2 (over core), cols: 4 (over z).
Axes of the slice: x: 2, y: 2, z: 4, core: 2. Of those that a mesh axis runs over, the one named last changes fastest.
Arguments:
- video: bfloat16 [8, 32, 64, 192], P('tm', 'rows', 'cols'), may hold values from -40 to 40, as said below
- cotangent: bfloat16 [8, 32, 64, 192], P('tm', 'rows', 'cols'), may hold values from -40 to 40, as said below
- weight: bfloat16 [5184, 192], P(('rows', 'cols')), may hold values from -0.078125 to 0.078125
- gain: float32 [192], replicated, may hold values from 0.25 to 1.75
- shift: float32 [192], replicated, may hold values from -3 to 3
- conv_bias: float32 [192], replicated, may hold values from -2 to 2
Outputs:
- output: bfloat16 [8, 32, 64, 192], P('tm', 'rows', 'cols')
- grad_video: bfloat16 [8, 32, 64, 192], P('tm', 'rows', 'cols')
- grad_weight: float32 [5184, 192], P(('rows', 'cols'))
- grad_gain: float32 [192], replicated
- grad_shift: float32 [192], replicated
- grad_conv_bias: float32 [192], replicated
The draws below stay inside these ranges and needn't reach their ends.
Inputs may be any that keep to these rules, and one draw needn't show every extreme that they name: `video`: Real-valued activations; their magnitude varies across frames, rows and columns. `cotangent`: Real-valued gradients; their magnitude varies across frames, rows and columns.
All inputs are finite; a program needn't handle non-finite values.
Results may differ from the reference program's by a relative error of at most 0.0031.
Values may be sent and summed in bfloat16 or wider, within the bound.
A program may use at most 64 MiB of HBM per device.

```python
import jax
import jax.numpy as jnp
from jax import lax

CH = 192
GROUPS = 32
FRAMES = 8
HEIGHT = 32
WIDTH = 64


def ramp_field():
    frame_pos = jnp.arange(FRAMES, dtype=jnp.float32).reshape(FRAMES, 1, 1, 1) / FRAMES
    row_pos = jnp.arange(HEIGHT, dtype=jnp.float32).reshape(1, HEIGHT, 1, 1) / HEIGHT
    col_pos = jnp.arange(WIDTH, dtype=jnp.float32).reshape(1, 1, WIDTH, 1) / WIDTH
    return jnp.exp(jnp.log(3.0) * (frame_pos + row_pos + col_pos - 1.5))


def frame_levels(key):
    level_key = jax.random.fold_in(key, 97)
    exponent = jax.random.uniform(level_key, (FRAMES,), jnp.float32, -0.6, 0.6)
    return jnp.exp(exponent).reshape(FRAMES, 1, 1, 1)


def field_draw(key):
    shape = (FRAMES, HEIGHT, WIDTH, CH)
    base_key = jax.random.fold_in(key, 5)
    base = jax.random.truncated_normal(base_key, -4.0, 4.0, shape, jnp.float32)
    return (base * ramp_field() * frame_levels(key)).astype(jnp.bfloat16)


def draw_video(key, part):
    return field_draw(jax.random.fold_in(key, 11))


def draw_cotangent(key, part):
    return field_draw(jax.random.fold_in(key, 23))


def level_of(stream_key, extent, cuts, low, top_value):
    level = 1.0
    for axis_at, parts in cuts:
        heights = jax.random.uniform(jax.random.fold_in(jax.random.fold_in(stream_key, 6), axis_at), (parts,), jnp.float32, low / len(cuts), top_value / len(cuts))
        level = level * jnp.repeat(jnp.exp(heights), extent[axis_at] // parts).reshape((-1,) + (1,) * (len(extent) - 1 - axis_at))
    return level


def normal_values(rng, dims, scale, bound, cuts=(), kind=jnp.bfloat16):
    values = scale * jax.random.normal(rng, dims, jnp.float32)
    if cuts:
        values = values * level_of(rng, dims, cuts, -0.22, 0.18)
    return jnp.clip(values, -bound, bound).astype(kind)


def setup_inputs(seed: int = 0) -> dict:
    key_list = jax.random.split(jax.random.key(seed), 7)
    return {
        "video": draw_video(jax.random.fold_in(key_list[6], 71), 0),
        "cotangent": draw_cotangent(jax.random.fold_in(key_list[6], 71), 0),
        "weight": normal_values(key_list[2], (27 * CH, CH), (27 * CH) ** -0.5, 0.078125, ((0, 8),)),
        "gain": jnp.clip(1.0 + 0.15 * jax.random.normal(key_list[3], (CH,), jnp.float32), 0.25, 1.75),
        "shift": normal_values(key_list[4], (CH,), 0.5, 3.0, (), jnp.float32),
        "conv_bias": normal_values(key_list[5], (CH,), 0.3, 2.0, (), jnp.float32),
    }


def per_group(values):
    return jnp.repeat(values.reshape(GROUPS, -1).sum(axis=1), CH // GROUPS)

def reference(video, cotangent, weight, gain, shift, conv_bias):
    video_f = video.astype(jnp.float32)
    count = float(FRAMES * HEIGHT * WIDTH * (CH // GROUPS))
    sums = lax.optimization_barrier(jnp.sum(video_f, axis=(0, 1, 2)))
    squares = lax.optimization_barrier(jnp.sum(video_f * video_f, axis=(0, 1, 2)))
    mean_c = per_group(sums) / count
    variance = per_group(squares) / count - mean_c * mean_c
    rstd_c = lax.rsqrt(variance + 1e-06)
    normed = (video_f - mean_c) * rstd_c
    pre = normed * gain + shift
    hidden = jax.nn.silu(pre).astype(jnp.bfloat16)
    padded = jnp.pad(hidden, ((2, 0), (1, 1), (1, 1), (0, 0))).astype(jnp.float32)
    grad_f = cotangent.astype(jnp.float32)
    grad_pad = jnp.pad(grad_f, ((0, 2), (1, 1), (1, 1), (0, 0)))
    kernel = weight.astype(jnp.float32).reshape(27, CH, CH)
    grad_flat = grad_f.reshape(-1, CH)
    total = jnp.zeros((FRAMES * HEIGHT * WIDTH, CH), jnp.float32) + conv_bias
    back_total = jnp.zeros((FRAMES * HEIGHT * WIDTH, CH), jnp.float32)
    kernel_grads = []
    for tap_t in range(3):
        for tap_r in range(3):
            for tap_c in range(3):
                index = (tap_t * 3 + tap_r) * 3 + tap_c
                window = padded[tap_t:tap_t + FRAMES, tap_r:tap_r + HEIGHT, tap_c:tap_c + WIDTH].reshape(-1, CH)
                total = total + jnp.dot(window, kernel[index])
                kernel_grads.append(jnp.dot(window.T, grad_flat))
                grad_win = grad_pad[2 - tap_t:2 - tap_t + FRAMES, 2 - tap_r:2 - tap_r + HEIGHT, 2 - tap_c:2 - tap_c + WIDTH].reshape(-1, CH)
                back_total = back_total + jnp.dot(grad_win, kernel[index].T)
    output = (video_f + total.reshape(FRAMES, HEIGHT, WIDTH, CH)).astype(jnp.bfloat16)
    grad_weight = jnp.stack(kernel_grads).reshape(27 * CH, CH)
    grad_hidden = lax.optimization_barrier(back_total.astype(jnp.bfloat16)).astype(jnp.float32)
    grad_hidden = grad_hidden.reshape(FRAMES, HEIGHT, WIDTH, CH)
    sigma = jax.nn.sigmoid(pre)
    grad_pre = grad_hidden * sigma * (1.0 + pre * (1.0 - sigma))
    grad_gain = lax.optimization_barrier(jnp.sum(grad_pre * normed, axis=(0, 1, 2)))
    grad_shift = lax.optimization_barrier(jnp.sum(grad_pre, axis=(0, 1, 2)))
    grad_conv_bias = lax.optimization_barrier(jnp.sum(grad_f, axis=(0, 1, 2)))
    term_a = per_group(gain * grad_shift) / count
    term_b = per_group(gain * grad_gain) / count
    grad_video = (grad_f + rstd_c * (grad_pre * gain - term_a - normed * term_b)).astype(jnp.bfloat16)
    return (output, grad_video, grad_weight, grad_gain, grad_shift, grad_conv_bias)
```

```python
import functools

import jax
import jax.numpy as jnp
from jax import lax
from jax.experimental import pallas as pl
from jax.experimental.pallas import tpu as pltpu
from jax.sharding import PartitionSpec as P

CH = 192
GROUPS = 32
MESH = pl.DeviceIdType.MESH


def greet(peers):
    barrier = pltpu.get_barrier_semaphore()
    for axis, count in peers:
        me = lax.axis_index(axis)
        for step in range(1, count):
            target = lax.rem(me + step, count)
            pl.semaphore_signal(barrier, inc=1, device_id={axis: target}, device_id_type=MESH)
    pl.semaphore_wait(barrier, sum(count - 1 for _, count in peers))


def sum_axis(value, axis, count, slots, send_sem, recv_sem):
    me = lax.axis_index(axis)
    slots[me] = value
    copies = []
    for step in range(1, count):
        target = lax.rem(me + step, count)
        copy = pltpu.make_async_remote_copy(
            src_ref=slots.at[me],
            dst_ref=slots.at[me],
            send_sem=send_sem.at[step - 1],
            recv_sem=recv_sem.at[step - 1],
            device_id={axis: target},
            device_id_type=MESH,
        )
        copy.start()
        copies.append(copy)
    for copy in copies:
        copy.wait()
    total = slots[0]
    for index in range(1, count):
        total = total + slots[index]
    return total


def sum_kernel(peers, value_ref, out_ref, *scratch):
    greet(peers)
    total = value_ref[...]
    for at, (axis, count) in enumerate(peers):
        total = sum_axis(total, axis, count, *scratch[3 * at : 3 * at + 3])
    out_ref[...] = total


def sum_all(value, peers, collective_id):
    scratch = []
    for _, count in peers:
        scratch += [
            pltpu.VMEM((count,) + value.shape, jnp.float32),
            pltpu.SemaphoreType.DMA((count - 1,)),
            pltpu.SemaphoreType.DMA((count - 1,)),
        ]
    return pl.pallas_call(
        functools.partial(sum_kernel, peers),
        out_shape=jax.ShapeDtypeStruct(value.shape, jnp.float32),
        in_specs=[pl.BlockSpec(memory_space=pltpu.VMEM)],
        out_specs=pl.BlockSpec(memory_space=pltpu.VMEM),
        scratch_shapes=scratch,
        compiler_params=pltpu.CompilerParams(collective_id=collective_id, has_side_effects=True),
        name="channel_sums",
    )(value)


def share_kernel(
    counts, g_ref, out_ref, near, out_t, in_t, out_c, in_c,
    near_send, near_recv, t_send, t_recv, c_send, c_recv, o_send, o_recv,
):
    tm, rows, cols = counts
    t, r, c = lax.axis_index("tm"), lax.axis_index("rows"), lax.axis_index("cols")
    greet((("tm", tm), ("rows", rows), ("cols", cols)))
    started = []

    def send(src, dst, send_sem, recv_sem, device):
        copy = pltpu.make_async_remote_copy(
            src_ref=src, dst_ref=dst, send_sem=send_sem, recv_sem=recv_sem,
            device_id=device, device_id_type=MESH,
        )
        copy.start()
        started.append(copy)
        return copy

    column = [lax.rem(c + 1 + i, cols) for i in range(cols)]
    near_copies = []
    for i in range(cols):
        near_copies.append([])
        for j in range(1, rows):
            target = lax.rem(r + j, rows)
            near_copies[i].append(send(
                g_ref.at[target, column[i]], near.at[j - 1, i],
                near_send.at[j - 1, i], near_recv.at[j - 1, i], {"rows": target},
            ))

    def near_sum(i, piece):
        total = g_ref[r, column[i], piece]
        for j in range(1, rows):
            total = total + near[j - 1, i, piece]
        return total

    t_copies = []
    for i in range(cols):
        for copy in near_copies[i]:
            copy.wait_recv()
        t_copies.append([])
        for j in range(1, tm):
            target = lax.rem(t + j, tm)
            out_t[i, j - 1] = near_sum(i, target).astype(jnp.bfloat16)
            t_copies[i].append(send(
                out_t.at[i, j - 1], in_t.at[i, j - 1],
                t_send.at[i, j - 1], t_recv.at[i, j - 1], {"tm": target},
            ))
    c_copies = []
    final = None
    for i in range(cols):
        for copy in t_copies[i]:
            copy.wait_recv()
        total = near_sum(i, t)
        for j in range(1, tm):
            total = total + in_t[i, j - 1].astype(jnp.float32)
        if i < cols - 1:
            out_c[i] = total.astype(jnp.bfloat16)
            c_copies.append(send(
                out_c.at[i], in_c.at[i], c_send.at[i], c_recv.at[i], {"cols": column[i]}
            ))
        else:
            final = total
    for i in range(cols - 1):
        c_copies[i].wait_recv()
        final = final + in_c[i].astype(jnp.float32)
    out_ref[t] = final
    o_copies = []
    for j in range(1, tm):
        target = lax.rem(t + j, tm)
        o_copies.append(send(
            out_ref.at[t], out_ref.at[t], o_send.at[j - 1], o_recv.at[j - 1], {"tm": target}
        ))
    for copy in o_copies:
        copy.wait_recv()
    for copy in started:
        copy.wait_send()


def share_sum(grads, counts, collective_id):
    tm, rows, cols = counts
    piece = grads.shape[3:]
    f32, bf16, dma = jnp.float32, jnp.bfloat16, pltpu.SemaphoreType.DMA
    return pl.pallas_call(
        functools.partial(share_kernel, counts),
        out_shape=jax.ShapeDtypeStruct((tm,) + piece, f32),
        in_specs=[pl.BlockSpec(memory_space=pltpu.VMEM)],
        out_specs=pl.BlockSpec(memory_space=pltpu.VMEM),
        scratch_shapes=[
            pltpu.VMEM((rows - 1, cols, tm) + piece, f32),
            pltpu.VMEM((cols, tm - 1) + piece, bf16),
            pltpu.VMEM((cols, tm - 1) + piece, bf16),
            pltpu.VMEM((cols - 1,) + piece, bf16),
            pltpu.VMEM((cols - 1,) + piece, bf16),
            dma((rows - 1, cols)), dma((rows - 1, cols)),
            dma((cols, tm - 1)), dma((cols, tm - 1)),
            dma((cols - 1,)), dma((cols - 1,)),
            dma((tm - 1,)), dma((tm - 1,)),
        ],
        compiler_params=pltpu.CompilerParams(
            collective_id=collective_id, has_side_effects=True, vmem_limit_bytes=40 << 20
        ),
        name="kernel_grad_sum",
    )(grads)


def padded_2(block, sides, width):
    for axis, dim in sides:
        count = lax.axis_size(axis)
        forward = [(i, i + 1) for i in range(count - 1)]
        backward = [(target, source) for source, target in forward]
        low = lax.ppermute(
            lax.slice_in_dim(block, block.shape[dim] - width, None, axis=dim), axis, forward
        )
        high = lax.ppermute(lax.slice_in_dim(block, 0, width, axis=dim), axis, backward)
        block = jnp.concatenate([low, block, high], axis=dim)
    return block


def per_group(values):
    return jnp.repeat(values.reshape(GROUPS, -1).sum(axis=1), CH // GROUPS)


def to_pairs(field, pair_count, local_rows, local_cols, channels):
    paired = field.reshape(pair_count, 2, local_rows, local_cols, channels)
    return paired.transpose(0, 2, 3, 1, 4).reshape(pair_count, local_rows, local_cols, 2 * channels)


def from_pairs(field, local_rows, local_cols, channels):
    pair_count = field.shape[0]
    split = field.reshape(pair_count, local_rows + 2, local_cols + 2, 2, channels)
    return split.transpose(0, 3, 1, 2, 4).reshape(
        2 * pair_count, local_rows + 2, local_cols + 2, channels
    )


def per_device(video, cotangent, weight, gain, shift, conv_bias):
    local_frames, local_rows, local_cols, channels = video.shape
    pair_count = local_frames // 2
    packed = jnp.concatenate(
        [
            to_pairs(video, pair_count, local_rows, local_cols, channels),
            to_pairs(cotangent, pair_count, local_rows, local_cols, channels),
        ],
        axis=-1,
    )
    framed = padded_2(packed, (("tm", 0), ("rows", 1), ("cols", 2)), 1)
    video_ext = from_pairs(
        framed[: pair_count + 1, :, :, : 2 * channels], local_rows, local_cols, channels
    )
    grad_ext = from_pairs(framed[1:, :, :, 2 * channels :], local_rows, local_cols, channels)
    video_f = video.astype(jnp.float32)
    tm, rows, cols = (lax.axis_size(axis) for axis in ("tm", "rows", "cols"))
    peers = (("rows", rows), ("tm", tm), ("cols", cols))
    moments = sum_all(
        jnp.stack([jnp.sum(video_f, axis=(0, 1, 2)), jnp.sum(video_f * video_f, axis=(0, 1, 2))]),
        peers, 0,
    )
    sums, squares = moments[0], moments[1]
    devices_all = lax.axis_size("tm") * lax.axis_size("rows") * lax.axis_size("cols")
    count = float(local_frames * local_rows * local_cols * devices_all * (channels // GROUPS))
    mean_c = per_group(sums) / count
    variance = per_group(squares) / count - mean_c * mean_c
    rstd_c = lax.rsqrt(variance + 1e-06)
    normed_ext = (video_ext.astype(jnp.float32) - mean_c) * rstd_c
    pre_ext = normed_ext * gain + shift
    frame_pos = lax.broadcasted_iota(jnp.int32, (local_frames + 2, 1, 1, 1), 0)
    row_pos = lax.broadcasted_iota(jnp.int32, (1, local_rows + 2, 1, 1), 1)
    col_pos = lax.broadcasted_iota(jnp.int32, (1, 1, local_cols + 2, 1), 2)
    time_index = lax.axis_index("tm")
    row_index = lax.axis_index("rows")
    col_index = lax.axis_index("cols")
    valid = (frame_pos >= 2) | (time_index > 0)
    valid = (
        valid
        & ((row_pos > 0) | (row_index > 0))
        & ((row_pos < local_rows + 1) | (row_index < lax.axis_size("rows") - 1))
    )
    valid = (
        valid
        & ((col_pos > 0) | (col_index > 0))
        & ((col_pos < local_cols + 1) | (col_index < lax.axis_size("cols") - 1))
    )
    padded = jnp.where(valid, jax.nn.silu(pre_ext), 0.0).astype(jnp.bfloat16)
    whole = lax.all_gather(weight, ("rows", "cols"), axis=0, tiled=True)
    cells = local_frames * local_rows * local_cols
    windows = []
    grad_windows = []
    for tap_t in range(3):
        for tap_r in range(3):
            for tap_c in range(3):
                windows.append(
                    padded[
                        tap_t : tap_t + local_frames,
                        tap_r : tap_r + local_rows,
                        tap_c : tap_c + local_cols,
                    ]
                )
                grad_windows.append(
                    grad_ext[
                        2 - tap_t : 2 - tap_t + local_frames,
                        2 - tap_r : 2 - tap_r + local_rows,
                        2 - tap_c : 2 - tap_c + local_cols,
                    ]
                )
    patches = jnp.concatenate(windows, axis=-1).reshape(cells, 27 * channels)
    grad_patches = jnp.concatenate(grad_windows, axis=-1).reshape(cells, 27 * channels)
    conv = jnp.dot(patches, whole, preferred_element_type=jnp.float32) + conv_bias
    output = (video_f + conv.reshape(local_frames, local_rows, local_cols, channels)).astype(
        jnp.bfloat16
    )
    grad_flat = cotangent.reshape(cells, channels)
    kernel_grad = lax.dot_general(
        grad_flat, patches, (((0,), (0,)), ((), ())), preferred_element_type=jnp.float32
    )
    kernel_grad = kernel_grad.reshape(tm, channels // tm, rows, cols, -1).transpose(2, 3, 0, 1, 4)
    grad_weight = share_sum(kernel_grad, (tm, rows, cols), 1).reshape(channels, -1).T
    flipped = (
        whole.reshape(27, channels, channels).transpose(0, 2, 1).reshape(27 * channels, channels)
    )
    grad_hidden = jnp.dot(grad_patches, flipped, preferred_element_type=jnp.float32).astype(
        jnp.bfloat16
    )
    grad_hidden = lax.optimization_barrier(grad_hidden).astype(jnp.float32)
    grad_hidden = grad_hidden.reshape(local_frames, local_rows, local_cols, channels)
    normed = normed_ext[2:, 1:-1, 1:-1]
    pre = pre_ext[2:, 1:-1, 1:-1]
    sigma = jax.nn.sigmoid(pre)
    grad_pre = grad_hidden * sigma * (1.0 + pre * (1.0 - sigma))
    grad_f = cotangent.astype(jnp.float32)
    gain_part = jnp.sum(grad_pre * normed, axis=(0, 1, 2))
    shift_part = jnp.sum(grad_pre, axis=(0, 1, 2))
    bias_part = jnp.sum(grad_f, axis=(0, 1, 2))
    totals = sum_all(jnp.stack([gain_part, shift_part, bias_part]), peers, 2)
    grad_gain, grad_shift, grad_conv_bias = totals[0], totals[1], totals[2]
    term_a = per_group(gain * grad_shift) / count
    term_b = per_group(gain * grad_gain) / count
    grad_video = (grad_f + rstd_c * (grad_pre * gain - term_a - normed * term_b)).astype(
        jnp.bfloat16
    )
    return (output, grad_video, grad_weight, grad_gain, grad_shift, grad_conv_bias)


def solution(mesh):
    return jax.shard_map(
        per_device,
        mesh=mesh,
        in_specs=(
            P("tm", "rows", "cols", None),
            P("tm", "rows", "cols", None),
            P(("rows", "cols"), None),
            P(),
            P(),
            P(),
        ),
        out_specs=(
            P("tm", "rows", "cols", None),
            P("tm", "rows", "cols", None),
            P(("rows", "cols"), None),
            P(),
            P(),
            P(),
        ),
        check_vma=False,
    )
```

```python
import functools

import jax
import jax.numpy as jnp
from jax import lax
from jax.experimental import pallas as pl
from jax.experimental.pallas import tpu as pltpu
from jax.sharding import PartitionSpec as P

CH = 192
GROUPS = 32
MESH = pl.DeviceIdType.MESH


def greet(peers):
    barrier = pltpu.get_barrier_semaphore()
    for axis, count in peers:
        me = lax.axis_index(axis)
        for step in range(1, count):
            target = lax.rem(me + step, count)
            pl.semaphore_signal(barrier, inc=1, device_id={axis: target}, device_id_type=MESH)
    pl.semaphore_wait(barrier, sum(count - 1 for _, count in peers))


def sum_axis(value, axis, count, slots, send_sem, recv_sem):
    me = lax.axis_index(axis)
    slots[me] = value
    copies = []
    for step in range(1, count):
        target = lax.rem(me + step, count)
        copy = pltpu.make_async_remote_copy(
            src_ref=slots.at[me],
            dst_ref=slots.at[me],
            send_sem=send_sem.at[step - 1],
            recv_sem=recv_sem.at[step - 1],
            device_id={axis: target},
            device_id_type=MESH,
        )
        copy.start()
        copies.append(copy)
    for copy in copies:
        copy.wait()
    total = slots[0]
    for index in range(1, count):
        total = total + slots[index]
    return total


def share_kernel(
    counts, cells_all, g_ref, parts_ref, pre_ref, video_ref, grad_ref, norm_ref, group_ref,
    out_ref, totals_ref, result_ref, near, out_t, in_t, out_c, in_c,
    near_send, near_recv, t_send, t_recv, c_send, c_recv, o_send, o_recv, *slots
):
    tm, rows, cols = counts
    t, r, c = lax.axis_index("tm"), lax.axis_index("rows"), lax.axis_index("cols")
    greet((("tm", tm), ("rows", rows), ("cols", cols)))
    started = []

    def send(src, dst, send_sem, recv_sem, device):
        copy = pltpu.make_async_remote_copy(
            src_ref=src, dst_ref=dst, send_sem=send_sem, recv_sem=recv_sem,
            device_id=device, device_id_type=MESH,
        )
        copy.start()
        started.append(copy)
        return copy

    column = [lax.rem(c + 1 + i, cols) for i in range(cols)]
    near_copies = []
    for i in range(cols):
        near_copies.append([])
        for j in range(1, rows):
            target = lax.rem(r + j, rows)
            near_copies[i].append(send(
                g_ref.at[target, column[i]], near.at[j - 1, i],
                near_send.at[j - 1, i], near_recv.at[j - 1, i], {"rows": target},
            ))

    def near_sum(i, piece):
        total = g_ref[r, column[i], piece]
        for j in range(1, rows):
            total = total + near[j - 1, i, piece]
        return total

    totals = sum_axis(parts_ref[...], "rows", rows, *slots[:3])
    t_copies = []
    for i in range(cols):
        for copy in near_copies[i]:
            copy.wait_recv()
        t_copies.append([])
        for j in range(1, tm):
            target = lax.rem(t + j, tm)
            out_t[i, j - 1] = near_sum(i, target).astype(jnp.bfloat16)
            t_copies[i].append(send(
                out_t.at[i, j - 1], in_t.at[i, j - 1],
                t_send.at[i, j - 1], t_recv.at[i, j - 1], {"tm": target},
            ))
    totals = sum_axis(totals, "tm", tm, *slots[3:6])
    c_copies = []
    final = None
    for i in range(cols):
        for copy in t_copies[i]:
            copy.wait_recv()
        total = near_sum(i, t)
        for j in range(1, tm):
            total = total + in_t[i, j - 1].astype(jnp.float32)
        if i < cols - 1:
            out_c[i] = total.astype(jnp.bfloat16)
            c_copies.append(send(
                out_c.at[i], in_c.at[i], c_send.at[i], c_recv.at[i], {"cols": column[i]}
            ))
        else:
            final = total
    totals = sum_axis(totals, "cols", cols, *slots[6:])
    totals_ref[...] = totals
    mean, rstd, gain = norm_ref[0:1], norm_ref[1:2], norm_ref[2:3]
    terms = jnp.dot(
        totals * gain, group_ref[...], precision=lax.Precision.HIGHEST,
        preferred_element_type=jnp.float32,
    ) / cells_all
    term_b, term_a = terms[0:1], terms[1:2]
    for i in range(cols - 1):
        c_copies[i].wait_recv()
        final = final + in_c[i].astype(jnp.float32)
    out_ref[t] = final
    o_copies = []
    for j in range(1, tm):
        target = lax.rem(t + j, tm)
        o_copies.append(send(
            out_ref.at[t], out_ref.at[t], o_send.at[j - 1], o_recv.at[j - 1], {"tm": target}
        ))

    @pl.loop(0, video_ref.shape[0])
    def _(f):
        @pl.loop(0, video_ref.shape[1])
        def _(row):
            normed = (video_ref[f, row].astype(jnp.float32) - mean) * rstd
            inner = pre_ref[f, row] * gain - term_a - normed * term_b
            result_ref[f, row] = (grad_ref[f, row].astype(jnp.float32) + rstd * inner).astype(jnp.bfloat16)

    for copy in o_copies:
        copy.wait_recv()
    for copy in started:
        copy.wait_send()


def slot_scratch(peers, shape):
    scratch = []
    for _, count in peers:
        scratch += [
            pltpu.VMEM((count,) + shape, jnp.float32),
            pltpu.SemaphoreType.DMA((count - 1,)),
            pltpu.SemaphoreType.DMA((count - 1,)),
        ]
    return scratch


def vmem(count):
    return [pl.BlockSpec(memory_space=pltpu.VMEM)] * count


def shaped(kind, *dims):
    return jax.ShapeDtypeStruct(dims, kind)


def share_sum(grads, parts, grad_pre, video, cotangent, norm, counts, cells_all, collective_id):
    tm, rows, cols = counts
    piece = grads.shape[3:]
    f32, bf16, dma = jnp.float32, jnp.bfloat16, pltpu.SemaphoreType.DMA
    member = lax.broadcasted_iota(jnp.int32, (CH, CH), 0) // (CH // GROUPS)
    other = lax.broadcasted_iota(jnp.int32, (CH, CH), 1) // (CH // GROUPS)
    group = (member == other).astype(f32)
    return pl.pallas_call(
        functools.partial(share_kernel, counts, cells_all),
        out_shape=(shaped(f32, tm, *piece), shaped(f32, *parts.shape), shaped(bf16, *video.shape)),
        in_specs=vmem(7),
        out_specs=tuple(vmem(3)),
        scratch_shapes=[
            pltpu.VMEM((rows - 1, cols, tm) + piece, f32),
            pltpu.VMEM((cols, tm - 1) + piece, bf16),
            pltpu.VMEM((cols, tm - 1) + piece, bf16),
            pltpu.VMEM((cols - 1,) + piece, bf16),
            pltpu.VMEM((cols - 1,) + piece, bf16),
            dma((rows - 1, cols)), dma((rows - 1, cols)),
            dma((cols, tm - 1)), dma((cols, tm - 1)),
            dma((cols - 1,)), dma((cols - 1,)),
            dma((tm - 1,)), dma((tm - 1,)),
        ] + slot_scratch((("rows", rows), ("tm", tm), ("cols", cols)), parts.shape),
        compiler_params=pltpu.CompilerParams(
            collective_id=collective_id, has_side_effects=True, vmem_limit_bytes=40 << 20
        ),
        name="kernel_grad_sum",
    )(grads, parts, grad_pre, video, cotangent, norm, group)


def halo_kernel(
    counts, video_ref, grad_ref, vside_ref, gside_ref, moments_ref,
    prev_ref, next_ref, vrow_ref, grow_ref, vcol_ref, gcol_ref, vcor_ref, gcor_ref, total_ref,
    vsides, gsides, send_sem, recv_sem, *slots
):
    tm, rows, cols = counts
    t, r, c = lax.axis_index("tm"), lax.axis_index("rows"), lax.axis_index("cols")
    greet((("tm", tm), ("rows", rows), ("cols", cols)))
    started = []

    def send(src, dst, axis, target):
        at = len(started)
        copy = pltpu.make_async_remote_copy(
            src_ref=src, dst_ref=dst, send_sem=send_sem.at[at], recv_sem=recv_sem.at[at],
            device_id={axis: target}, device_id_type=MESH,
        )
        copy.start()
        started.append(copy)
        return copy

    up, down = lax.rem(t + 1, tm), lax.rem(t + tm - 1, tm)
    side_copies = [
        send(vside_ref, vsides.at[0], "tm", up), send(gside_ref, gsides.at[1], "tm", down)
    ]
    block_copies = [send(video_ref, prev_ref, "tm", up), send(grad_ref, next_ref, "tm", down)]
    last_row = video_ref.shape[1] - 1
    after, before = lax.rem(r + 1, rows), lax.rem(r + rows - 1, rows)
    row_copies = [
        send(video_ref.at[:, last_row], vrow_ref.at[0, 1], "rows", after),
        send(video_ref.at[:, 0], vrow_ref.at[1, 1], "rows", before),
        send(grad_ref.at[:, last_row], grow_ref.at[0, 0], "rows", after),
        send(grad_ref.at[:, 0], grow_ref.at[1, 0], "rows", before),
    ]
    vsides[1] = vside_ref[...]
    gsides[0] = gside_ref[...]
    total = sum_axis(moments_ref[...], "tm", tm, *slots[:3])
    for copy in side_copies:
        copy.wait_recv()
    right, left = lax.rem(c + 1, cols), lax.rem(c + cols - 1, cols)
    col_copies = []
    for sides, col_ref in ((vsides, vcol_ref), (gsides, gcol_ref)):
        col_copies.append(send(sides.at[:, 1], col_ref.at[0], "cols", right))
        col_copies.append(send(sides.at[:, 0], col_ref.at[1], "cols", left))
    total = sum_axis(total, "cols", cols, *slots[3:6])
    for copy in col_copies:
        copy.wait_recv()
    for col_ref, cor_ref in ((vcol_ref, vcor_ref), (gcol_ref, gcor_ref)):
        row_copies.append(send(col_ref, cor_ref.at[0], "rows", after))
        row_copies.append(send(col_ref, cor_ref.at[1], "rows", before))
    total_ref[...] = sum_axis(total, "rows", rows, *slots[6:])
    for copy in block_copies:
        copy.wait_recv()
    for block, row_ref, at in ((prev_ref, vrow_ref, 0), (next_ref, grow_ref, 1)):
        row_copies.append(send(block.at[:, last_row], row_ref.at[0, at], "rows", after))
        row_copies.append(send(block.at[:, 0], row_ref.at[1, at], "rows", before))
    for copy in row_copies:
        copy.wait_recv()
    for copy in started:
        copy.wait_send()


def halo(video, cotangent, moments, counts, collective_id):
    tm, rows, cols = counts
    frames, height, width, channels = video.shape
    f32, bf16, dma = jnp.float32, jnp.bfloat16, pltpu.SemaphoreType.DMA
    sides = [jnp.stack([field[:, :, 0], field[:, :, -1]]) for field in (video, cotangent)]
    row = shaped(bf16, 2, 2, frames, width, channels)
    col = shaped(bf16, 2, 2, frames, height, channels)
    cor = shaped(bf16, 2, 2, 2, frames, height, channels)
    block = shaped(bf16, *video.shape)
    held = pltpu.VMEM((2, 2, frames, height, channels), bf16)
    return pl.pallas_call(
        functools.partial(halo_kernel, counts),
        out_shape=(block, block, row, row, col, col, cor, cor, shaped(f32, *moments.shape)),
        in_specs=vmem(5),
        out_specs=tuple(vmem(9)),
        scratch_shapes=[held, held, dma((20,)), dma((20,))]
        + slot_scratch((("tm", tm), ("cols", cols), ("rows", rows)), moments.shape),
        compiler_params=pltpu.CompilerParams(
            collective_id=collective_id, has_side_effects=True, vmem_limit_bytes=24 << 20
        ),
        name="halo",
    )(video, cotangent, *sides, moments)


def fill(wide, shifted, blocks, row_ref, col_ref, cor_ref, apply, edge):
    frames, height, width, _ = blocks[0].shape
    low, top, left, high, bottom, right = edge

    def keep(value, good):
        return jnp.where(good, apply(value.astype(jnp.float32)), 0.0)

    for at in range(2):
        whole = (low, high)[at]
        for f in range(frames):
            frame = at * frames + f

            @pl.loop(0, height, unroll=4)
            def _(i):
                wide[frame, i + 1, 8 : 8 + width] = keep(blocks[at][f, i], whole)

            for side in range(2):
                row, row_good = ((0, top), (height + 1, bottom))[side]
                wide[frame, row, 8 : 8 + width] = keep(row_ref[side, at, f], whole & row_good)
                col, col_good = ((7, left), (8 + width, right))[side]
                strip = keep(col_ref[side, at, f], whole & col_good)
                for i in range(height):
                    wide[frame, i + 1, col : col + 1] = strip[i : i + 1]
                for end in range(2):
                    row, row_good = ((0, top), (height + 1, bottom))[end]
                    corner = keep(cor_ref[end, side, at, f], whole & col_good & row_good)
                    pick = (height - 1, 0)[end]
                    wide[frame, row, col : col + 1] = corner[pick : pick + 1]

    @pl.loop(0, 2 * frames)
    def _(frame):
        @pl.loop(0, height + 2, unroll=3)
        def _(i):
            for shift in range(3):
                shifted[shift, frame, i] = wide[frame, i, 7 + shift : 7 + shift + width].astype(jnp.bfloat16)


def hidden_kernel(
    counts, video_ref, prev_ref, vrow_ref, vcol_ref, vcor_ref,
    grad_ref, next_ref, grow_ref, gcol_ref, gcor_ref, norm_ref,
    hid_ref, cot_ref, out_ref, wide, turned
):
    tm, rows, cols = counts
    t, r, c = lax.axis_index("tm"), lax.axis_index("rows"), lax.axis_index("cols")
    frames, height, width, channels = video_ref.shape
    mean, rstd, gain, shift = (norm_ref[i : i + 1] for i in range(4))
    top, bottom, left, right = r > 0, r < rows - 1, c > 0, c < cols - 1

    def activate(value):
        pre = (value - mean) * rstd * gain + shift
        return pre / (1.0 + jnp.exp(-pre))

    always = t >= 0
    fill(wide, hid_ref, (prev_ref, video_ref), vrow_ref, vcol_ref, vcor_ref, activate,
         (t > 0, top, left, always, bottom, right))
    fill(wide, cot_ref, (grad_ref, next_ref), grow_ref, gcol_ref, gcor_ref, lambda value: value,
         (always, top, left, t < tm - 1, bottom, right))
    cells = frames * height * width
    turned[...] = grad_ref[...].reshape(cells, channels).T
    depth = 27 * channels // (rows * cols)
    piece = channels // tm
    grads = {}
    for chunk in range(rows * cols):
        first, last = chunk * depth, (chunk + 1) * depth
        parts = []
        for tap in range(first // channels, (last - 1) // channels + 1):
            if tap not in grads:
                a, b, s = tap // 9, tap // 3 % 3, tap % 3
                window = hid_ref[s, a : a + frames, b : b + height].reshape(cells, channels)
                grads = {tap: jnp.dot(turned[...], window, preferred_element_type=jnp.float32)}
            start = max(first - tap * channels, 0)
            stop = min(last - tap * channels, channels)
            parts.append(grads[tap][:, start:stop])
        joined = jnp.concatenate(parts, axis=1)
        for i in range(tm):
            out_ref[chunk // cols, chunk % cols, i] = joined[i * piece : (i + 1) * piece]


def hidden_and_kernel_grad(video, cotangent, around, norm, counts):
    tm, rows, cols = counts
    frames, height, width, channels = video.shape
    prev, after, vrow, grow, vcol, gcol, vcor, gcor = around
    f32, bf16 = jnp.float32, jnp.bfloat16
    shifts = shaped(bf16, 3, 2 * frames, height + 2, width, channels)
    depth = 27 * channels // (rows * cols)
    return pl.pallas_call(
        functools.partial(hidden_kernel, counts),
        out_shape=(shifts, shifts, shaped(f32, rows, cols, tm, channels // tm, depth)),
        in_specs=vmem(11),
        out_specs=tuple(vmem(3)),
        scratch_shapes=[
            pltpu.VMEM((2 * frames, height + 2, width + 16, channels), f32),
            pltpu.VMEM((channels, frames * height * width), bf16),
        ],
        compiler_params=pltpu.CompilerParams(vmem_limit_bytes=40 << 20),
        name="hidden",
    )(video, prev, vrow, vcol, vcor, cotangent, after, grow, gcol, gcor, norm)


def conv_kernel(hid_ref, cot_ref, weight_ref, video_ref, grad_ref, norm_ref, bias_ref,
                out_ref, pre_ref, parts_ref, total):
    frames, height, width, channels = video_ref.shape
    cells = frames * height * width
    f32 = jnp.float32
    back = jnp.zeros((cells, channels), f32)
    for tap in range(27):
        a, b, s = 2 - tap // 9, 2 - tap // 3 % 3, 2 - tap % 3
        window = cot_ref[s, a : a + frames, b : b + height].reshape(cells, channels)
        back = back + lax.dot_general(
            window, weight_ref[tap], (((1,), (1,)), ((), ())), preferred_element_type=f32
        )
    total[...] = back.astype(jnp.bfloat16).astype(f32).reshape(frames, height, width, channels)
    mean, rstd, gain, shift = (norm_ref[i : i + 1] for i in range(4))

    def step(at, sums):
        f, i = at // height, at % height
        normed = (video_ref[f, i].astype(f32) - mean) * rstd
        pre = normed * gain + shift
        sigma = 1.0 / (1.0 + jnp.exp(-pre))
        grad_pre = total[f, i] * sigma * (1.0 + pre * (1.0 - sigma))
        pre_ref[f, i] = grad_pre
        grad = grad_ref[f, i].astype(f32)
        return (sums[0] + grad_pre * normed, sums[1] + grad_pre, sums[2] + grad)

    zero = jnp.zeros((width, channels), f32)
    sums = lax.fori_loop(0, frames * height, step, (zero, zero, zero))
    for i in range(3):
        parts_ref[i : i + 1] = jnp.sum(sums[i], axis=0, keepdims=True)
    parts_ref[3:] = jnp.zeros((5, channels), f32)
    conv = jnp.zeros((cells, channels), f32)
    for tap in range(27):
        a, b, s = tap // 9, tap // 3 % 3, tap % 3
        window = hid_ref[s, a : a + frames, b : b + height].reshape(cells, channels)
        conv = conv + jnp.dot(window, weight_ref[tap], preferred_element_type=f32)
    conv = (conv + bias_ref[...]).reshape(frames, height, width, channels)
    out_ref[...] = (video_ref[...].astype(f32) + conv).astype(jnp.bfloat16)


def convolve(hid, cot, weight, video, cotangent, norm, bias):
    f32, bf16 = jnp.float32, jnp.bfloat16
    return pl.pallas_call(
        conv_kernel,
        out_shape=(shaped(bf16, *video.shape), shaped(f32, *video.shape), shaped(f32, 8, CH)),
        in_specs=vmem(7),
        out_specs=tuple(vmem(3)),
        scratch_shapes=[pltpu.VMEM(video.shape, f32)],
        compiler_params=pltpu.CompilerParams(vmem_limit_bytes=40 << 20),
        name="convolve",
    )(hid, cot, weight, video, cotangent, norm, bias)


def per_group(values):
    return jnp.repeat(values.reshape(GROUPS, -1).sum(axis=1), CH // GROUPS)


def per_device(video, cotangent, weight, gain, shift, conv_bias):
    channels = video.shape[-1]
    counts = tuple(lax.axis_size(axis) for axis in ("tm", "rows", "cols"))
    whole = lax.all_gather(weight, ("rows", "cols"), axis=0, tiled=True).reshape(27, channels, channels)
    video_f = video.astype(jnp.float32)
    moments = jnp.stack(
        [jnp.sum(video_f, axis=(0, 1, 2)), jnp.sum(video_f * video_f, axis=(0, 1, 2))]
    )
    *around, sums = halo(video, cotangent, moments, counts, 0)
    count = float(video.size // channels * counts[0] * counts[1] * counts[2] * (channels // GROUPS))
    mean_c = per_group(sums[0]) / count
    variance = per_group(sums[1]) / count - mean_c * mean_c
    norm = jnp.stack([mean_c, lax.rsqrt(variance + 1e-06), gain, shift])
    hid, cot, kernel_grad = hidden_and_kernel_grad(video, cotangent, around, norm, counts)
    output, grad_pre, parts = convolve(
        hid, cot, whole, video, cotangent, norm, conv_bias.reshape(1, channels)
    )
    grad_weight, totals, grad_video = share_sum(
        kernel_grad, parts, grad_pre, video, cotangent, norm, counts, count, 1
    )
    grad_weight = grad_weight.reshape(channels, -1).T
    return (output, grad_video, grad_weight, totals[0], totals[1], totals[2])


def solution(mesh):
    return jax.shard_map(
        per_device,
        mesh=mesh,
        in_specs=(
            P("tm", "rows", "cols", None),
            P("tm", "rows", "cols", None),
            P(("rows", "cols"), None),
            P(),
            P(),
            P(),
        ),
        out_specs=(
            P("tm", "rows", "cols", None),
            P("tm", "rows", "cols", None),
            P(("rows", "cols"), None),
            P(),
            P(),
            P(),
        ),
        check_vma=False,
    )
```

```python
import functools

import jax
import jax.numpy as jnp
from jax import lax
from jax.experimental import pallas as pl
from jax.experimental.pallas import tpu as pltpu
from jax.sharding import PartitionSpec as P

CH = 192
GROUPS = 32
MESH = pl.DeviceIdType.MESH


def greet(peers):
    barrier = pltpu.get_barrier_semaphore()
    for axis, count in peers:
        me = lax.axis_index(axis)
        for step in range(1, count):
            target = lax.rem(me + step, count)
            pl.semaphore_signal(barrier, inc=1, device_id={axis: target}, device_id_type=MESH)
    pl.semaphore_wait(barrier, sum(count - 1 for _, count in peers))


def sum_axis(value, axis, count, slots, send_sem, recv_sem):
    me = lax.axis_index(axis)
    slots[me] = value
    copies = []
    for step in range(1, count):
        target = lax.rem(me + step, count)
        copy = pltpu.make_async_remote_copy(
            src_ref=slots.at[me],
            dst_ref=slots.at[me],
            send_sem=send_sem.at[step - 1],
            recv_sem=recv_sem.at[step - 1],
            device_id={axis: target},
            device_id_type=MESH,
        )
        copy.start()
        copies.append(copy)
    for copy in copies:
        copy.wait()
    total = slots[0]
    for index in range(1, count):
        total = total + slots[index]
    return total


def share_kernel(
    counts, cells_all, g_ref, parts_ref, pre_ref, video_ref, grad_ref, norm_ref, group_ref,
    out_ref, totals_ref, result_ref, near, out_t, in_t, out_c, in_c,
    near_send, near_recv, t_send, t_recv, c_send, c_recv, o_send, o_recv, *slots
):
    tm, rows, cols = counts
    t, r, c = lax.axis_index("tm"), lax.axis_index("rows"), lax.axis_index("cols")
    greet((("tm", tm), ("rows", rows), ("cols", cols)))
    started = []

    def send(src, dst, send_sem, recv_sem, device):
        copy = pltpu.make_async_remote_copy(
            src_ref=src, dst_ref=dst, send_sem=send_sem, recv_sem=recv_sem,
            device_id=device, device_id_type=MESH,
        )
        copy.start()
        started.append(copy)
        return copy

    column = [lax.rem(c + 1 + i, cols) for i in range(cols)]
    near_copies = []
    for i in range(cols):
        near_copies.append([])
        for j in range(1, rows):
            target = lax.rem(r + j, rows)
            near_copies[i].append(send(
                g_ref.at[target, column[i]], near.at[j - 1, i],
                near_send.at[j - 1, i], near_recv.at[j - 1, i], {"rows": target},
            ))

    def near_sum(i, piece):
        total = g_ref[r, column[i], piece]
        for j in range(1, rows):
            total = total + near[j - 1, i, piece]
        return total

    totals = sum_axis(parts_ref[...], "rows", rows, *slots[:3])
    t_copies = []
    for i in range(cols):
        for copy in near_copies[i]:
            copy.wait_recv()
        t_copies.append([])
        for j in range(1, tm):
            target = lax.rem(t + j, tm)
            out_t[i, j - 1] = near_sum(i, target).astype(jnp.bfloat16)
            t_copies[i].append(send(
                out_t.at[i, j - 1], in_t.at[i, j - 1],
                t_send.at[i, j - 1], t_recv.at[i, j - 1], {"tm": target},
            ))
    totals = sum_axis(totals, "tm", tm, *slots[3:6])
    c_copies = []
    final = None
    for i in range(cols):
        for copy in t_copies[i]:
            copy.wait_recv()
        total = near_sum(i, t)
        for j in range(1, tm):
            total = total + in_t[i, j - 1].astype(jnp.float32)
        if i < cols - 1:
            out_c[i] = total.astype(jnp.bfloat16)
            c_copies.append(send(
                out_c.at[i], in_c.at[i], c_send.at[i], c_recv.at[i], {"cols": column[i]}
            ))
        else:
            final = total
    totals = sum_axis(totals, "cols", cols, *slots[6:])
    totals_ref[...] = totals
    mean, rstd, gain = norm_ref[0:1], norm_ref[1:2], norm_ref[2:3]
    terms = jnp.dot(
        totals * gain, group_ref[...], precision=lax.Precision.HIGHEST,
        preferred_element_type=jnp.float32,
    ) / cells_all
    term_b, term_a = terms[0:1], terms[1:2]
    for i in range(cols - 1):
        c_copies[i].wait_recv()
        final = final + in_c[i].astype(jnp.float32)
    out_ref[t] = final
    o_copies = []
    for j in range(1, tm):
        target = lax.rem(t + j, tm)
        o_copies.append(send(
            out_ref.at[t], out_ref.at[t], o_send.at[j - 1], o_recv.at[j - 1], {"tm": target}
        ))

    @pl.loop(0, video_ref.shape[0])
    def _(f):
        @pl.loop(0, video_ref.shape[1])
        def _(row):
            normed = (video_ref[f, row].astype(jnp.float32) - mean) * rstd
            inner = pre_ref[f, row] * gain - term_a - normed * term_b
            result_ref[f, row] = (grad_ref[f, row].astype(jnp.float32) + rstd * inner).astype(jnp.bfloat16)

    for copy in o_copies:
        copy.wait_recv()
    for copy in started:
        copy.wait_send()


def slot_scratch(peers, shape):
    scratch = []
    for _, count in peers:
        scratch += [
            pltpu.VMEM((count,) + shape, jnp.float32),
            pltpu.SemaphoreType.DMA((count - 1,)),
            pltpu.SemaphoreType.DMA((count - 1,)),
        ]
    return scratch


def vmem(count):
    return [pl.BlockSpec(memory_space=pltpu.VMEM)] * count


def shaped(kind, *dims):
    return jax.ShapeDtypeStruct(dims, kind)


def share_sum(grads, parts, grad_pre, video, cotangent, norm, counts, cells_all, collective_id):
    tm, rows, cols = counts
    piece = grads.shape[3:]
    f32, bf16, dma = jnp.float32, jnp.bfloat16, pltpu.SemaphoreType.DMA
    return pl.pallas_call(
        functools.partial(share_kernel, counts, cells_all),
        out_shape=(shaped(f32, tm, *piece), shaped(f32, *parts.shape), shaped(bf16, *video.shape)),
        in_specs=vmem(7),
        out_specs=tuple(vmem(3)),
        scratch_shapes=[
            pltpu.VMEM((rows - 1, cols, tm) + piece, f32),
            pltpu.VMEM((cols, tm - 1) + piece, bf16),
            pltpu.VMEM((cols, tm - 1) + piece, bf16),
            pltpu.VMEM((cols - 1,) + piece, bf16),
            pltpu.VMEM((cols - 1,) + piece, bf16),
            dma((rows - 1, cols)), dma((rows - 1, cols)),
            dma((cols, tm - 1)), dma((cols, tm - 1)),
            dma((cols - 1,)), dma((cols - 1,)),
            dma((tm - 1,)), dma((tm - 1,)),
        ] + slot_scratch((("rows", rows), ("tm", tm), ("cols", cols)), parts.shape),
        compiler_params=pltpu.CompilerParams(
            collective_id=collective_id, has_side_effects=True, vmem_limit_bytes=28 << 20
        ),
        name="kernel_grad_sum",
    )(grads, parts, grad_pre, video, cotangent, norm, group_matrix())


def halo_kernel(
    counts, cells_all, video_ref, grad_ref, vside_ref, gside_ref, affine_ref, group_ref,
    prev_ref, next_ref, vrow_ref, grow_ref, vcol_ref, gcol_ref, vcor_ref, gcor_ref, norm_ref,
    vsides, gsides, send_sem, recv_sem, *slots
):
    tm, rows, cols = counts
    t, r, c = lax.axis_index("tm"), lax.axis_index("rows"), lax.axis_index("cols")
    greet((("tm", tm), ("rows", rows), ("cols", cols)))
    started = []

    def send(src, dst, axis, target):
        at = len(started)
        copy = pltpu.make_async_remote_copy(
            src_ref=src, dst_ref=dst, send_sem=send_sem.at[at], recv_sem=recv_sem.at[at],
            device_id={axis: target}, device_id_type=MESH,
        )
        copy.start()
        started.append(copy)
        return copy

    up, down = lax.rem(t + 1, tm), lax.rem(t + tm - 1, tm)
    side_copies = [
        send(vside_ref, vsides.at[0], "tm", up), send(gside_ref, gsides.at[1], "tm", down)
    ]
    block_copies = [send(video_ref, prev_ref, "tm", up), send(grad_ref, next_ref, "tm", down)]
    last_row = video_ref.shape[1] - 1
    after, before = lax.rem(r + 1, rows), lax.rem(r + rows - 1, rows)
    row_copies = [
        send(video_ref.at[:, last_row], vrow_ref.at[0, 1], "rows", after),
        send(video_ref.at[:, 0], vrow_ref.at[1, 1], "rows", before),
        send(grad_ref.at[:, last_row], grow_ref.at[0, 0], "rows", after),
        send(grad_ref.at[:, 0], grow_ref.at[1, 0], "rows", before),
    ]
    vsides[1] = vside_ref[...]
    gsides[0] = gside_ref[...]
    height, width, channels = video_ref.shape[1:]

    def moment(at, sums):
        value = video_ref[at // height, at % height].astype(jnp.float32)
        return (sums[0] + value, sums[1] + value * value)

    zero = jnp.zeros((width, channels), jnp.float32)
    sums = lax.fori_loop(0, video_ref.shape[0] * height, moment, (zero, zero), unroll=4)
    moments = jnp.concatenate(
        [jnp.sum(value, axis=0, keepdims=True) for value in sums]
        + [jnp.zeros((6, channels), jnp.float32)], axis=0,
    )
    total = sum_axis(moments, "tm", tm, *slots[:3])
    for copy in side_copies:
        copy.wait_recv()
    right, left = lax.rem(c + 1, cols), lax.rem(c + cols - 1, cols)
    col_copies = []
    for sides, col_ref in ((vsides, vcol_ref), (gsides, gcol_ref)):
        col_copies.append(send(sides.at[:, 1], col_ref.at[0], "cols", right))
        col_copies.append(send(sides.at[:, 0], col_ref.at[1], "cols", left))
    total = sum_axis(total, "cols", cols, *slots[3:6])
    for copy in col_copies:
        copy.wait_recv()
    for col_ref, cor_ref in ((vcol_ref, vcor_ref), (gcol_ref, gcor_ref)):
        row_copies.append(send(col_ref, cor_ref.at[0], "rows", after))
        row_copies.append(send(col_ref, cor_ref.at[1], "rows", before))
    total = sum_axis(total, "rows", rows, *slots[6:])
    means = jnp.dot(
        total, group_ref[...], precision=lax.Precision.HIGHEST, preferred_element_type=jnp.float32
    ) / cells_all
    mean = means[0:1]
    norm_ref[0:1] = mean
    norm_ref[1:2] = lax.rsqrt(means[1:2] - mean * mean + 1e-06)
    norm_ref[2:4] = affine_ref[...]
    for copy in block_copies:
        copy.wait_recv()
    for block, row_ref, at in ((prev_ref, vrow_ref, 0), (next_ref, grow_ref, 1)):
        row_copies.append(send(block.at[:, last_row], row_ref.at[0, at], "rows", after))
        row_copies.append(send(block.at[:, 0], row_ref.at[1, at], "rows", before))
    for copy in row_copies:
        copy.wait_recv()
    for copy in started:
        copy.wait_send()


def group_matrix():
    member = lax.broadcasted_iota(jnp.int32, (CH, CH), 0) // (CH // GROUPS)
    other = lax.broadcasted_iota(jnp.int32, (CH, CH), 1) // (CH // GROUPS)
    return (member == other).astype(jnp.float32)


def halo(video, cotangent, affine, counts, cells_all, collective_id):
    tm, rows, cols = counts
    frames, height, width, channels = video.shape
    f32, bf16, dma = jnp.float32, jnp.bfloat16, pltpu.SemaphoreType.DMA
    sides = [jnp.stack([field[:, :, 0], field[:, :, -1]]) for field in (video, cotangent)]
    row = shaped(bf16, 2, 2, frames, width, channels)
    col = shaped(bf16, 2, 2, frames, height, channels)
    cor = shaped(bf16, 2, 2, 2, frames, height, channels)
    block = shaped(bf16, *video.shape)
    held = pltpu.VMEM((2, 2, frames, height, channels), bf16)
    return pl.pallas_call(
        functools.partial(halo_kernel, counts, cells_all),
        out_shape=(block, block, row, row, col, col, cor, cor, shaped(f32, 4, channels)),
        in_specs=vmem(6),
        out_specs=tuple(vmem(9)),
        scratch_shapes=[held, held, dma((20,)), dma((20,))]
        + slot_scratch((("tm", tm), ("cols", cols), ("rows", rows)), (8, channels)),
        compiler_params=pltpu.CompilerParams(
            collective_id=collective_id, has_side_effects=True, vmem_limit_bytes=24 << 20
        ),
        name="halo",
    )(video, cotangent, *sides, affine, group_matrix())


def fill(wide, shifted, blocks, row_ref, col_ref, cor_ref, apply, edge):
    frames, height, width, _ = blocks[0].shape
    low, top, left, high, bottom, right = edge

    def keep(value, good):
        return jnp.where(good, apply(value.astype(jnp.float32)), 0.0)

    for at in range(2):
        whole = (low, high)[at]
        for f in range(frames):
            frame = at * frames + f

            @pl.loop(0, height, unroll=4)
            def _(i):
                wide[frame, i + 1, 8 : 8 + width] = keep(blocks[at][f, i], whole)

            for side in range(2):
                row, row_good = ((0, top), (height + 1, bottom))[side]
                wide[frame, row, 8 : 8 + width] = keep(row_ref[side, at, f], whole & row_good)
                col, col_good = ((7, left), (8 + width, right))[side]
                strip = keep(col_ref[side, at, f], whole & col_good)
                for i in range(height):
                    wide[frame, i + 1, col : col + 1] = strip[i : i + 1]
                for end in range(2):
                    row, row_good = ((0, top), (height + 1, bottom))[end]
                    corner = keep(cor_ref[end, side, at, f], whole & col_good & row_good)
                    pick = (height - 1, 0)[end]
                    wide[frame, row, col : col + 1] = corner[pick : pick + 1]

    @pl.loop(0, 2 * frames)
    def _(frame):
        @pl.loop(0, height + 2, unroll=3)
        def _(i):
            for shift in range(3):
                shifted[shift, frame, i] = wide[frame, i, 7 + shift : 7 + shift + width].astype(jnp.bfloat16)


def hidden_kernel(
    counts, video_ref, prev_ref, vrow_ref, vcol_ref, vcor_ref,
    grad_ref, next_ref, grow_ref, gcol_ref, gcor_ref, norm_ref, weight_ref, bias_ref,
    out_ref, result_ref, pre_ref, parts_ref, hid_ref, cot_ref, wide, turned, total
):
    tm, rows, cols = counts
    t, r, c = lax.axis_index("tm"), lax.axis_index("rows"), lax.axis_index("cols")
    frames, height, width, channels = video_ref.shape
    mean, rstd, gain, shift = (norm_ref[i : i + 1] for i in range(4))
    top, bottom, left, right = r > 0, r < rows - 1, c > 0, c < cols - 1

    def activate(value):
        pre = (value - mean) * rstd * gain + shift
        return pre / (1.0 + jnp.exp(-pre))

    always = t >= 0
    fill(wide, hid_ref, (prev_ref, video_ref), vrow_ref, vcol_ref, vcor_ref, activate,
         (t > 0, top, left, always, bottom, right))
    fill(wide, cot_ref, (grad_ref, next_ref), grow_ref, gcol_ref, gcor_ref, lambda value: value,
         (always, top, left, t < tm - 1, bottom, right))
    cells = frames * height * width
    turned[...] = grad_ref[...].reshape(cells, channels).T
    depth = 27 * channels // (rows * cols)
    piece = channels // tm
    grads = {}
    for chunk in range(rows * cols):
        first, last = chunk * depth, (chunk + 1) * depth
        parts = []
        for tap in range(first // channels, (last - 1) // channels + 1):
            if tap not in grads:
                a, b, s = tap // 9, tap // 3 % 3, tap % 3
                window = hid_ref[s, a : a + frames, b : b + height].reshape(cells, channels)
                grads = {tap: jnp.dot(turned[...], window, preferred_element_type=jnp.float32)}
            start = max(first - tap * channels, 0)
            stop = min(last - tap * channels, channels)
            parts.append(grads[tap][:, start:stop])
        joined = jnp.concatenate(parts, axis=1)
        for i in range(tm):
            out_ref[chunk // cols, chunk % cols, i] = joined[i * piece : (i + 1) * piece]
    backward(cot_ref, weight_ref, video_ref, grad_ref, norm_ref, pre_ref, parts_ref, total)
    forward(hid_ref, weight_ref, video_ref, bias_ref, result_ref)


def local_work(video, cotangent, around, norm, weight, bias, counts):
    tm, rows, cols = counts
    frames, height, width, channels = video.shape
    prev, after, vrow, grow, vcol, gcol, vcor, gcor = around
    f32, bf16 = jnp.float32, jnp.bfloat16
    shifts = pltpu.VMEM((3, 2 * frames, height + 2, width, channels), bf16)
    depth = 27 * channels // (rows * cols)
    return pl.pallas_call(
        functools.partial(hidden_kernel, counts),
        out_shape=(
            shaped(f32, rows, cols, tm, channels // tm, depth),
            shaped(bf16, *video.shape), shaped(f32, *video.shape), shaped(f32, 8, channels),
        ),
        in_specs=vmem(13),
        out_specs=tuple(vmem(4)),
        scratch_shapes=[
            shifts, shifts,
            pltpu.VMEM((2 * frames, height + 2, width + 16, channels), f32),
            pltpu.VMEM((channels, frames * height * width), bf16),
            pltpu.VMEM(video.shape, f32),
        ],
        compiler_params=pltpu.CompilerParams(vmem_limit_bytes=28 << 20),
        name="local_work",
    )(video, prev, vrow, vcol, vcor, cotangent, after, grow, gcol, gcor, norm, weight, bias)


def backward(cot_ref, weight_ref, video_ref, grad_ref, norm_ref, pre_ref, parts_ref, total):
    frames, height, width, channels = video_ref.shape
    cells = frames * height * width
    f32 = jnp.float32
    back = jnp.zeros((cells, channels), f32)
    for tap in range(27):
        a, b, s = 2 - tap // 9, 2 - tap // 3 % 3, 2 - tap % 3
        window = cot_ref[s, a : a + frames, b : b + height].reshape(cells, channels)
        back = back + lax.dot_general(
            window, weight_ref[tap], (((1,), (1,)), ((), ())), preferred_element_type=f32
        )
    total[...] = back.astype(jnp.bfloat16).astype(f32).reshape(frames, height, width, channels)
    mean, rstd, gain, shift = (norm_ref[i : i + 1] for i in range(4))

    def step(at, sums):
        f, i = at // height, at % height
        normed = (video_ref[f, i].astype(f32) - mean) * rstd
        pre = normed * gain + shift
        sigma = 1.0 / (1.0 + jnp.exp(-pre))
        grad_pre = total[f, i] * sigma * (1.0 + pre * (1.0 - sigma))
        pre_ref[f, i] = grad_pre
        grad = grad_ref[f, i].astype(f32)
        return (sums[0] + grad_pre * normed, sums[1] + grad_pre, sums[2] + grad)

    zero = jnp.zeros((width, channels), f32)
    sums = lax.fori_loop(0, frames * height, step, (zero, zero, zero))
    for i in range(3):
        parts_ref[i : i + 1] = jnp.sum(sums[i], axis=0, keepdims=True)
    parts_ref[3:] = jnp.zeros((5, channels), f32)


def forward(hid_ref, weight_ref, video_ref, bias_ref, out_ref):
    frames, height, width, channels = video_ref.shape
    cells = frames * height * width
    f32 = jnp.float32
    conv = jnp.zeros((cells, channels), f32)
    for tap in range(27):
        a, b, s = tap // 9, tap // 3 % 3, tap % 3
        window = hid_ref[s, a : a + frames, b : b + height].reshape(cells, channels)
        conv = conv + jnp.dot(window, weight_ref[tap], preferred_element_type=f32)
    conv = (conv + bias_ref[...]).reshape(frames, height, width, channels)
    out_ref[...] = (video_ref[...].astype(f32) + conv).astype(jnp.bfloat16)


def per_device(video, cotangent, weight, gain, shift, conv_bias):
    channels = video.shape[-1]
    counts = tuple(lax.axis_size(axis) for axis in ("tm", "rows", "cols"))
    whole = lax.all_gather(weight, ("rows", "cols"), axis=0, tiled=True).reshape(27, channels, channels)
    count = float(video.size // channels * counts[0] * counts[1] * counts[2] * (channels // GROUPS))
    *around, norm = halo(video, cotangent, jnp.stack([gain, shift]), counts, count, 0)
    kernel_grad, output, grad_pre, parts = local_work(
        video, cotangent, around, norm, whole, conv_bias.reshape(1, channels), counts
    )
    grad_weight, totals, grad_video = share_sum(
        kernel_grad, parts, grad_pre, video, cotangent, norm, counts, count, 1
    )
    grad_weight = grad_weight.reshape(channels, -1).T
    return (output, grad_video, grad_weight, totals[0], totals[1], totals[2])


def solution(mesh):
    return jax.shard_map(
        per_device,
        mesh=mesh,
        in_specs=(
            P("tm", "rows", "cols", None),
            P("tm", "rows", "cols", None),
            P(("rows", "cols"), None),
            P(),
            P(),
            P(),
        ),
        out_specs=(
            P("tm", "rows", "cols", None),
            P("tm", "rows", "cols", None),
            P(("rows", "cols"), None),
            P(),
            P(),
            P(),
        ),
        check_vma=False,
    )
```
